32 devices in a mesh: mode: 8 (over z, y), space: 4 (over x, core).
Axes of the slice: x: 2, y: 2, z: 4, core: 2. Of those that a mesh axis runs over, the one named last changes fastest.
Arguments:
- pressure: float32 [512, 8, 4, 128], P('mode', 'space'), may hold values from -6 to 6
- source: float32 [512, 8, 4, 128], P('mode', 'space'), may hold values from -6 to 6
- coefficients: float32 [32, 8, 4, 128], P(None, 'space'), may hold values from 0.2 to 2
- coupling: float32 [32, 512, 512], P(None, 'mode'), as said below
Outputs:
- pressure_out: float32 [512, 8, 4, 128], P('mode', 'space')
- residual: float32 [512, 8, 4, 128], P('mode', 'space')
The draws below stay inside these ranges and needn't reach their ends.
Inputs may be any that keep to these rules, and one draw needn't show every extreme that they name: coupling[k] is symmetric for every k.
All inputs are finite; a program needn't handle non-finite values.
Results may differ from the reference program's by a relative error of at most 0.00011.
Values sent between devices are 32-bit elements; how exact they have to be, the bound alone decides.
No kernel may reach another device: no remote copies, remote signals or barrier semaphores. Data moves between devices by JAX's collectives and lax.ppermute only.
A program may use at most 64 MiB of HBM per device.

```python
import math
import jax
import jax.numpy as jnp
from jax import lax

P_SIZE = 512
TERMS = 32
ITERS = 2
CY = 4
CZ = 128
NX = 8


def draw_coupling(key, part):
    raw = jax.random.normal(key, (TERMS, P_SIZE, P_SIZE), jnp.float32)
    symmetric = (raw + jnp.swapaxes(raw, 1, 2)) * (0.5 / jnp.sqrt(2.0 * P_SIZE))
    rows = lax.broadcasted_iota(jnp.int32, (TERMS, P_SIZE, P_SIZE), 1)
    cols = lax.broadcasted_iota(jnp.int32, (TERMS, P_SIZE, P_SIZE), 2)
    terms = lax.broadcasted_iota(jnp.int32, (TERMS, P_SIZE, P_SIZE), 0)
    identity = jnp.where((rows == cols) & (terms == 0), 1.0, 0.0).astype(jnp.float32)
    return symmetric + identity


def block_levels(key, shape, shards, low, largest):
    level = 1.0
    for position, shards_of in shards:
        heights = jax.random.uniform(jax.random.fold_in(jax.random.fold_in(key, 6), position), (shards_of,), jnp.float32, low / len(shards), largest / len(shards))
        level = level * jnp.repeat(jnp.exp(heights), shape[position] // shards_of).reshape((-1,) + (1,) * (len(shape) - 1 - position))
    return level


def normal_values(stream_key, shape, scale, most, split=(), dtype=jnp.bfloat16):
    drawn = jax.random.normal(stream_key, shape, jnp.float32) * scale
    if len(split) > 0:
        drawn = block_levels(stream_key, shape, split, -0.22, 0.18) * drawn
    return jnp.clip(drawn, min=-most, max=most).astype(dtype)


def setup_inputs(seed: int = 0) -> dict:
    arg_keys = jax.random.split(jax.random.key(seed), 5)
    pressure = normal_values(arg_keys[0], (P_SIZE, NX, CY, CZ), 1.0, 6.0, ((0, 8), (1, 4)), jnp.float32)
    source = normal_values(arg_keys[1], (P_SIZE, NX, CY, CZ), 1.0, 6.0, ((0, 8), (1, 4)), jnp.float32)
    coefficients = jnp.clip(jnp.exp(math.log(2.0) - 2.3025851 * jax.random.uniform(arg_keys[2], (TERMS, NX, CY, CZ), jnp.float32) ** block_levels(arg_keys[2], (TERMS, NX, CY, CZ), ((1, 4),), -0.2, 0.2)), 0.2, 2.0)
    coupling = draw_coupling(jax.random.fold_in(arg_keys[4], 71), 0)
    return {"pressure": pressure, "source": source, "coefficients": coefficients, "coupling": coupling}


storage_coef = 1.0
damping = 0.7


def shifted(padded, spatial_axis, offset):
    index = [slice(None)] * padded.ndim
    for place in (-3, -2, -1):
        index[place] = slice(1, padded.shape[place] - 1)
    index[spatial_axis] = slice(1 + offset, padded.shape[spatial_axis] - 1 + offset)
    return padded[tuple(index)]


def yz_pad(array):
    return jnp.pad(array, [(0, 0)] * (array.ndim - 2) + [(1, 1), (1, 1)])


def local_stencil(coef_x, field_x):
    coef_p = yz_pad(coef_x)
    field_p = yz_pad(field_x)
    centre_c = shifted(coef_p, -3, 0)
    centre_f = shifted(field_p, -3, 0)
    total = None
    for spatial_axis in (-3, -2, -1):
        for offset in (-1, 1):
            term = 0.5 * (centre_c + shifted(coef_p, spatial_axis, offset)) * (centre_f - shifted(field_p, spatial_axis, offset))
            total = term if total is None else total + term
    return total


def face_total(coef_x):
    coef_p = yz_pad(coef_x)
    centre_c = shifted(coef_p, -3, 0)
    total = jnp.zeros(centre_c.shape, jnp.float32)
    for spatial_axis in (-3, -2, -1):
        for offset in (-1, 1):
            total = total + 0.5 * (centre_c + shifted(coef_p, spatial_axis, offset))
    return total


def x_pad(array):
    return jnp.pad(array, [(0, 0), (1, 1), (0, 0), (0, 0)])


def reference(pressure, source, coefficients, coupling):
    coef_x = x_pad(coefficients)
    mean_x = coef_x[0]
    diag = storage_coef + face_total(mean_x)
    residual = source
    for outer in range(ITERS):
        press_x = x_pad(pressure)

        def add_term(total, inputs):
            coef_k, matrix = inputs
            mixed = jnp.einsum('ij,jxyz->ixyz', matrix, press_x, precision=lax.Precision.HIGHEST)
            return total + local_stencil(coef_k[None], mixed), None

        applied = lax.scan(add_term, jnp.zeros(pressure.shape, jnp.float32), (coef_x, coupling))[0]
        residual = source - storage_coef * pressure - applied
        first = damping * residual / diag
        mean_apply = storage_coef * first + local_stencil(mean_x[None], x_pad(first))
        second = first + damping * (residual - mean_apply) / diag
        pressure = pressure + second
    return pressure, residual
```

```python
import jax
import jax.numpy as jnp
from jax import lax
from jax.experimental import pallas as pl
from jax.experimental.pallas import tpu as pltpu
from jax.sharding import PartitionSpec as P

ITERS = 2
LANES = 128
KINDS = 6

storage_coef = 1.0
damping = 0.7

VMEM = pl.BlockSpec(memory_space=pltpu.VMEM)
SMEM = pl.BlockSpec(memory_space=pltpu.SMEM)


def split_kernel(c_ref, out_ref):
    x = c_ref[...]
    width = x.shape[1]
    hi = x.astype(jnp.bfloat16)
    lo = (x - hi.astype(jnp.float32)).astype(jnp.bfloat16)
    out_ref[:, 0:width] = hi
    out_ref[:, width : 2 * width] = hi
    out_ref[:, 2 * width : 3 * width] = lo


def split_coupling(c):
    rows, width = c.shape
    step = rows // 8
    return pl.pallas_call(
        split_kernel,
        grid=(rows // step,),
        in_specs=[pl.BlockSpec((step, width), lambda i: (i, 0))],
        out_specs=pl.BlockSpec((step, 3 * width), lambda i: (i, 0)),
        out_shape=jax.ShapeDtypeStruct((rows, 3 * width), jnp.bfloat16),
        compiler_params=pltpu.CompilerParams(vmem_limit_bytes=16 * 2**20),
        cost_estimate=pl.CostEstimate(flops=0, bytes_accessed=10 * rows * width, transcendentals=0),
    )(c)


def lane_shift(x, offset):
    moved = pltpu.roll(x, (-offset) % LANES, 1)
    lane = lax.broadcasted_iota(jnp.int32, x.shape, 1)
    edge = 0 if offset < 0 else LANES - 1
    return jnp.where(lane == edge, 0.0, moved)


def mix_plane(offsets, blocks, c_ref, w_ref, field_ref, u_ref, m_ref):
    block_rows, cells = blocks[0].shape
    modes = c_ref.shape[1] // 3
    terms = w_ref.shape[1]
    own = c_ref.shape[0] // terms
    for s, block in enumerate(blocks):
        x = block[...]
        hi = x.astype(jnp.bfloat16)
        lo = (x - hi.astype(jnp.float32)).astype(jnp.bfloat16)
        row = pl.multiple_of(offsets[s], block_rows)
        u_ref[pl.ds(row, block_rows), :] = hi
        u_ref[pl.ds(row + modes, block_rows), :] = lo
        u_ref[pl.ds(row + 2 * modes, block_rows), :] = hi
    tile = m_ref.shape[2]
    group = min(32, own)
    for t in range(cells // tile):
        m_ref[t] = jnp.dot(
            c_ref[...], u_ref[:, t * tile : (t + 1) * tile], preferred_element_type=jnp.float32
        )
        for r in range(tile // LANES):
            lanes = slice(t * tile + r * LANES, t * tile + (r + 1) * LANES)
            for g in range(own // group):
                total = [None] * KINDS
                for k in range(terms):
                    m = m_ref[t, k * own + g * group : k * own + (g + 1) * group, r * LANES : (r + 1) * LANES]
                    for n in range(KINDS):
                        term = w_ref[n, k : k + 1, lanes] * m
                        total[n] = term if total[n] is None else total[n] + term
                for n in range(KINDS):
                    field_ref[n, g * group : (g + 1) * group, lanes] = total[n]


def plane_flux(field_ref, rows):
    sums = []
    for r in range(rows):
        lanes = slice(r * LANES, (r + 1) * LANES)
        total = field_ref[2, :, lanes] + field_ref[3, :, lanes]
        if r > 0:
            total = total - field_ref[3, :, (r - 1) * LANES : r * LANES]
        if r < rows - 1:
            total = total - field_ref[2, :, (r + 1) * LANES : (r + 2) * LANES]
        below, above = field_ref[4, :, lanes], field_ref[5, :, lanes]
        total = total + (below - lane_shift(above, -1)) + (above - lane_shift(below, 1))
        sums.append(total)
    return sums


def mix_kernel(count, offsets, *refs):
    blocks = refs[:count]
    c_ref, w_ref, s_ref, lower_ref, upper_ref, field_ref, u_ref, m_ref = refs[count:]
    mix_plane(offsets, blocks, c_ref, w_ref, field_ref, u_ref, m_ref)
    rows = s_ref.shape[1] // LANES
    for r, total in enumerate(plane_flux(field_ref, rows)):
        s_ref[:, r * LANES : (r + 1) * LANES] = total
    lower_ref[...] = field_ref[0]
    upper_ref[...] = field_ref[1]


def mix(offsets, blocks, c, w):
    own = blocks[0].shape[0]
    cells = blocks[0].shape[1]
    modes = c.shape[1] // 3
    tile = 2 * LANES if cells % (2 * LANES) == 0 else LANES
    shape = jax.ShapeDtypeStruct((own, cells), jnp.float32)
    return pl.pallas_call(
        lambda *refs: mix_kernel(len(blocks), *refs),
        in_specs=[SMEM] + [VMEM] * (len(blocks) + 2),
        out_specs=[VMEM] * 3,
        out_shape=[shape] * 3,
        scratch_shapes=[
            pltpu.VMEM((KINDS, own, cells), jnp.float32),
            pltpu.VMEM((3 * modes, cells), jnp.bfloat16),
            pltpu.VMEM((cells // tile, c.shape[0], tile), jnp.float32),
        ],
        compiler_params=pltpu.CompilerParams(vmem_limit_bytes=28 * 2**20),
        cost_estimate=pl.CostEstimate(
            flops=2 * c.shape[0] * c.shape[1] * cells, bytes_accessed=2 * c.size, transcendentals=0
        ),
    )(offsets, *blocks, c, w)


def assemble(mixed, press, source):
    planes = len(mixed)
    parts = []
    for p in range(planes):
        s, lower, upper = mixed[p]
        total = source[p] - storage_coef * press[p] - s - lower - upper
        if p > 0:
            total = total + mixed[p - 1][2]
        if p < planes - 1:
            total = total + mixed[p + 1][1]
        parts.append(total)
    return parts


def smooth_kernel(planes, last, *refs):
    parts, press = refs[:planes], refs[planes : 2 * planes]
    low_in, high_in, lower, upper, w_ref, inv_ref = refs[2 * planes : 2 * planes + 6]
    outs = refs[2 * planes + 6 :]
    rows = lower.shape[1] // LANES

    def row(r):
        return slice(r * LANES, (r + 1) * LANES)

    res, first = {}, {}
    for r in range(rows):
        for p in range(planes):
            value = parts[p][:, row(r)]
            if p == 0:
                value = value + low_in[1, :, row(r)]
            if p == planes - 1:
                value = value + high_in[1, :, row(r)]
            res[p, r] = value
        res[-1, r] = low_in[0, :, row(r)] + lower[:, row(r)]
        res[planes, r] = high_in[0, :, row(r)] + upper[:, row(r)]
        for p in range(-1, planes + 1):
            first[p, r] = inv_ref[p + 1 : p + 2, row(r)] * res[p, r]
    for p in range(planes):
        for r in range(rows):
            f = first[p, r]

            def w(n):
                return w_ref[p * KINDS + n : p * KINDS + n + 1, row(r)]

            mean = storage_coef * f + w(0) * (f - first[p - 1, r]) + w(1) * (f - first[p + 1, r])
            mean = mean + w(2) * (f - first[p, r - 1] if r > 0 else f)
            mean = mean + w(3) * (f - first[p, r + 1] if r < rows - 1 else f)
            mean = mean + w(4) * (f - lane_shift(f, -1)) + w(5) * (f - lane_shift(f, 1))
            second = f + inv_ref[p + 1 : p + 2, row(r)] * (res[p, r] - mean)
            new = press[p][:, row(r)] + second
            if last:
                outs[0][:, p * rows + r, :] = new
                outs[1][:, p * rows + r, :] = res[p, r]
            else:
                outs[p][:, row(r)] = new


def smooth(parts, press, low_in, high_in, lower, upper, w0, inv, last):
    planes = len(parts)
    own, cells = lower.shape
    if last:
        out_shape = [jax.ShapeDtypeStruct((own, planes * cells // LANES, LANES), jnp.float32)] * 2
    else:
        out_shape = [jax.ShapeDtypeStruct((own, cells), jnp.float32)] * planes
    return pl.pallas_call(
        lambda *refs: smooth_kernel(planes, last, *refs),
        in_specs=[VMEM] * (2 * planes + 6),
        out_specs=[VMEM] * len(out_shape),
        out_shape=out_shape,
        compiler_params=pltpu.CompilerParams(vmem_limit_bytes=16 * 2**20),
        cost_estimate=pl.CostEstimate(flops=40 * own * cells * planes, bytes_accessed=0, transcendentals=0),
    )(*parts, *press, low_in, high_in, lower, upper, w0, inv)


def edge_weights(coef, low, high):
    ext = jnp.concatenate([low[:, None], coef, high[:, None]], axis=1)
    pad = jnp.pad(coef, [(0, 0), (0, 0), (1, 1), (1, 1)])
    near = [
        ext[:, :-2],
        ext[:, 2:],
        pad[:, :, :-2, 1:-1],
        pad[:, :, 2:, 1:-1],
        pad[:, :, 1:-1, :-2],
        pad[:, :, 1:-1, 2:],
    ]
    return jnp.stack([0.5 * (coef + n) for n in near])


def gathered(block, inner, outer):
    size = inner * outer
    ring = [(i, (i + inner) % size) for i in range(size)]
    blocks, current = [], block
    for step in range(outer):
        blocks.append(current)
        other = current
        for turn in range(1, inner):
            swap = [(i, i // inner * inner + (i % inner + 1) % inner) for i in range(size)]
            other = lax.ppermute(other, "mode", swap)
            blocks.append(other)
        if step < outer - 1:
            current = lax.ppermute(current, "mode", ring)
    return blocks


def on_device(pressure, source, coefficients, coupling):
    size, slabs = lax.axis_size("mode"), lax.axis_size("space")
    inner = 2 if size % 2 == 0 else 1
    outer = size // inner
    own, planes, cy, cz = pressure.shape
    cells = cy * cz
    terms = coefficients.shape[0]
    up = [(i, i + 1) for i in range(slabs - 1)]
    down = [(j, i) for i, j in up]

    press = [pressure[:, p].reshape(own, cells) for p in range(planes)]
    blocks = [gathered(u, inner, outer) for u in press]

    mode_at = lax.axis_index("mode")
    outer_at, inner_at = mode_at // inner, mode_at % inner
    offsets = jnp.stack(
        [
            ((outer_at - step + outer) % outer * inner + (inner_at - turn + inner) % inner) * own
            for step in range(outer)
            for turn in range(inner)
        ]
    ).astype(jnp.int32)

    c = split_coupling(coupling.reshape(terms * own, size * own))

    low = lax.ppermute(jnp.concatenate([coefficients[:, planes - 1], coefficients[:1, planes - 2]]), "space", up)
    high = lax.ppermute(jnp.concatenate([coefficients[:, 0], coefficients[:1, 1]]), "space", down)
    weights = edge_weights(coefficients, low[:terms], high[:terms])
    w = [weights[:, :, p].reshape(KINDS, terms, cells) for p in range(planes)]
    w0 = jnp.concatenate([weights[:, 0, p].reshape(KINDS, cells) for p in range(planes)])
    mean = jnp.concatenate([low[None, 0], coefficients[0], high[None, 0]])
    faces = edge_weights(mean[None], low[terms:], high[terms:])[:, 0].sum(axis=0)
    at = lax.axis_index("space") * planes - 1 + jnp.arange(planes + 2)
    inside = ((at >= 0) & (at < slabs * planes))[:, None]
    inv = jnp.where(inside, (damping / (storage_coef + faces)).reshape(planes + 2, cells), 0.0)

    src = [source[:, p].reshape(own, cells) for p in range(planes)]
    for step in range(ITERS):
        mixed = [mix(offsets, blocks[p], c, w[p]) for p in range(planes)]
        parts = assemble(mixed, press, src)
        lower, upper = mixed[0][1], mixed[planes - 1][2]
        low_in = lax.ppermute(jnp.stack([parts[planes - 1], upper]), "space", up)
        high_in = lax.ppermute(jnp.stack([parts[0], lower]), "space", down)
        last = step == ITERS - 1
        outs = smooth(parts, press, low_in, high_in, lower, upper, w0, inv, last)
        if not last:
            press = outs
            blocks = [gathered(u, inner, outer) for u in press]
    return tuple(x.reshape(pressure.shape) for x in outs)


def solution(mesh):
    in_specs = (
        P("mode", "space", None, None),
        P("mode", "space", None, None),
        P(None, "space", None, None),
        P(None, "mode", None),
    )
    out_specs = (P("mode", "space", None, None), P("mode", "space", None, None))
    return jax.shard_map(
        on_device, mesh=mesh, in_specs=in_specs, out_specs=out_specs, check_vma=False
    )
```

```python
import jax
import jax.numpy as jnp
from jax import lax
from jax.experimental import pallas as pl
from jax.experimental.pallas import tpu as pltpu
from jax.sharding import PartitionSpec as P

ITERS = 2
LANES = 128
KINDS = 6

storage_coef = 1.0
damping = 0.7

VMEM = pl.BlockSpec(memory_space=pltpu.VMEM)
SMEM = pl.BlockSpec(memory_space=pltpu.SMEM)


def parts_of(x):
    hi = x.astype(jnp.bfloat16)
    return hi, (x - hi.astype(jnp.float32)).astype(jnp.bfloat16)


def place(u_ref, blocks, offsets):
    part = u_ref.shape[0] // 3
    for s, block in enumerate(blocks):
        rows = block.shape[0]
        hi, lo = parts_of(block[...])
        row = pl.multiple_of(offsets[s], rows)
        u_ref[pl.ds(row, rows), :] = hi
        u_ref[pl.ds(row + part, rows), :] = lo
        u_ref[pl.ds(row + 2 * part, rows), :] = hi


def lane_shift(x, offset):
    moved = pltpu.roll(x, (-offset) % LANES, 1)
    lane = lax.broadcasted_iota(jnp.int32, x.shape, 1)
    edge = 0 if offset < 0 else LANES - 1
    return jnp.where(lane == edge, 0.0, moved)


def mix_kernel(planes, half, count, odd, offsets, *refs):
    blocks, refs = refs[:count], refs[count:]
    c_ref, w_ref, press, source, part_ref, odd_ref, even_ref, field_ref, u_ref, cs_ref, sems = refs
    rows, lanes_all = press.shape
    cells = lanes_all // planes
    terms = w_ref.shape[1]
    chunk = terms // sems.shape[0]

    copies = [
        pltpu.make_async_copy(
            c_ref.at[pl.ds(k, chunk), half], cs_ref.at[pl.ds(k, chunk)], sems.at[k // chunk]
        )
        for k in range(0, terms, chunk)
    ]
    for copy in copies:
        copy.start()
    place(u_ref, blocks, offsets)
    tile = 2 * LANES if cells % (2 * LANES) == 0 else LANES

    def product(k, t):
        hi, lo = parts_of(cs_ref[k : k + chunk].reshape(chunk * rows, cs_ref.shape[2]))
        return jnp.dot(
            jnp.concatenate([hi, hi, lo], axis=1),
            u_ref[:, t * tile : (t + 1) * tile],
            preferred_element_type=jnp.float32,
        )

    def weigh(start, t, m):
        for r in range(tile // LANES):
            lanes = slice(t * tile + r * LANES, t * tile + (r + 1) * LANES)
            total = [None if start == 0 else field_ref[n, :, lanes] for n in range(KINDS)]
            for k in range(chunk):
                value = m[k * rows : (k + 1) * rows, r * LANES : (r + 1) * LANES]
                for n in range(KINDS):
                    term = w_ref[n, start + k : start + k + 1, lanes] * value
                    total[n] = term if total[n] is None else total[n] + term
            for n in range(KINDS):
                field_ref[n, :, lanes] = total[n]

    before = None
    for k in range(0, terms, chunk):
        copies[k // chunk].wait()
        for t in range(lanes_all // tile):
            m = product(k, t)
            if before is not None:
                weigh(*before)
            before = (k, t, m)
    weigh(*before)

    count = cells // LANES
    for p in range(planes):
        for r in range(count):

            def field(n, p=p, r=r):
                return field_ref[n, :, p * cells + r * LANES : p * cells + (r + 1) * LANES]

            lanes = slice(p * cells + r * LANES, p * cells + (r + 1) * LANES)
            flux = field(0) + field(1) + field(2) + field(3)
            if p > 0:
                flux = flux - field(1, p - 1, r)
            if p < planes - 1:
                flux = flux - field(0, p + 1, r)
            if r > 0:
                flux = flux - field(3, p, r - 1)
            if r < count - 1:
                flux = flux - field(2, p, r + 1)
            below, above = field(4), field(5)
            flux = flux + (below - lane_shift(above, -1)) + (above - lane_shift(below, 1))
            part_ref[:, lanes] = source[:, lanes] - storage_coef * press[:, lanes] - flux

    lower, upper = slice(0, cells), slice((planes - 1) * cells, planes * cells)
    is_odd = odd[0] == 1
    for at, (low, high) in enumerate(
        [(part_ref[:, lower], part_ref[:, upper]), (field_ref[0, :, lower], field_ref[1, :, upper])]
    ):
        odd_ref[at] = jnp.where(is_odd, high, low)
        even_ref[at] = jnp.where(is_odd, low, high)


def mix(odd, offsets, blocks, c, w, press, source, half, planes):
    rows, lanes_all = press.shape
    cells = lanes_all // planes
    terms, _, _, modes = c.shape
    chunks = max(1, terms * rows // 256)
    sent = jax.ShapeDtypeStruct((2, rows, cells), jnp.float32)
    return pl.pallas_call(
        lambda *refs: mix_kernel(planes, half, len(blocks), *refs),
        in_specs=[SMEM] * 2 + [VMEM] * len(blocks) + [pl.BlockSpec(memory_space=pltpu.HBM)] + [VMEM] * 3,
        out_specs=[VMEM] * 3,
        out_shape=[jax.ShapeDtypeStruct(press.shape, jnp.float32), sent, sent],
        scratch_shapes=[
            pltpu.VMEM((KINDS, rows, lanes_all), jnp.float32),
            pltpu.VMEM((3 * modes, lanes_all), jnp.bfloat16),
            pltpu.VMEM((terms, rows, modes), jnp.float32),
            pltpu.SemaphoreType.DMA((chunks,)),
        ],
        compiler_params=pltpu.CompilerParams(vmem_limit_bytes=20 * 2**20),
        cost_estimate=pl.CostEstimate(
            flops=6 * terms * rows * modes * lanes_all, bytes_accessed=4 * terms * rows * modes, transcendentals=0
        ),
    )(odd, offsets, *blocks, c, w, press, source)


def smooth_kernel(planes, halves, final, odd, *refs):
    w_ref, inv_ref = refs[6 * halves : 6 * halves + 2]
    outs = refs[6 * halves + 2 :]
    is_odd = odd[0] == 1
    for h in range(halves):
        part, press, odd_own, even_own, odd_in, even_in = refs[6 * h : 6 * h + 6]
        rows, lanes_all = press.shape
        cells = lanes_all // planes
        count = cells // LANES

        def lanes(p, r):
            return slice(p * cells + r * LANES, p * cells + (r + 1) * LANES)

        res, first = {}, {}
        for r in range(count):
            row = slice(r * LANES, (r + 1) * LANES)
            for p in range(planes):
                res[p, r] = part[:, lanes(p, r)]
            res[0, r] = res[0, r] + jnp.where(is_odd, even_in[1, :, row], odd_in[1, :, row])
            res[planes - 1, r] = res[planes - 1, r] + jnp.where(is_odd, odd_in[1, :, row], even_in[1, :, row])
            odd_side = odd_in[0, :, row] + odd_own[1, :, row]
            even_side = even_in[0, :, row] + even_own[1, :, row]
            res[-1, r] = jnp.where(is_odd, even_side, odd_side)
            res[planes, r] = jnp.where(is_odd, odd_side, even_side)
            for p in range(-1, planes + 1):
                first[p, r] = inv_ref[p + 1 : p + 2, row] * res[p, r]
        for p in range(planes):
            for r in range(count):
                f = first[p, r]
                row = slice(r * LANES, (r + 1) * LANES)

                def w(n):
                    return w_ref[n : n + 1, lanes(p, r)]

                mean = storage_coef * f + w(0) * (f - first[p - 1, r]) + w(1) * (f - first[p + 1, r])
                mean = mean + w(2) * (f - first[p, r - 1] if r > 0 else f)
                mean = mean + w(3) * (f - first[p, r + 1] if r < count - 1 else f)
                mean = mean + w(4) * (f - lane_shift(f, -1)) + w(5) * (f - lane_shift(f, 1))
                second = f + inv_ref[p + 1 : p + 2, row] * (res[p, r] - mean)
                new = press[:, lanes(p, r)] + second
                if final:
                    outs[0][h * rows : (h + 1) * rows, p * count + r, :] = new
                    outs[1][h * rows : (h + 1) * rows, p * count + r, :] = res[p, r]
                else:
                    outs[h][:, lanes(p, r)] = new


def smooth(odd, states, w0, inv, final):
    halves = len(states)
    rows, lanes_all = states[0][1].shape
    planes = inv.shape[0] - 2
    if final:
        out_shape = [jax.ShapeDtypeStruct((halves * rows, lanes_all // LANES, LANES), jnp.float32)] * 2
    else:
        out_shape = [jax.ShapeDtypeStruct((rows, lanes_all), jnp.float32)] * halves
    return pl.pallas_call(
        lambda *refs: smooth_kernel(planes, halves, final, *refs),
        in_specs=[SMEM] + [VMEM] * (6 * halves + 2),
        out_specs=[VMEM] * len(out_shape),
        out_shape=out_shape,
        compiler_params=pltpu.CompilerParams(vmem_limit_bytes=8 * 2**20),
        cost_estimate=pl.CostEstimate(flops=40 * halves * rows * lanes_all, bytes_accessed=0, transcendentals=0),
    )(odd, *[x for state in states for x in state], w0, inv)


def weights_kernel(beside, coef_ref, low_ref, high_ref, w_ref, w0_ref, inv_ref):
    terms = coef_ref.shape[0]
    rows = low_ref.shape[1]
    planes = coef_ref.shape[1] // rows
    a = {(p, r): coef_ref[:, p * rows + r, :] for p in range(planes) for r in range(rows)}
    a.update({(-1, r): low_ref[0:terms, r, :] for r in range(rows)})
    a.update({(planes, r): high_ref[0:terms, r, :] for r in range(rows)})
    beyond = {(-2, r): low_ref[terms : terms + 1, r, :] for r in range(rows)}
    beyond.update({(planes + 1, r): high_ref[terms : terms + 1, r, :] for r in range(rows)})

    def near(x, p, r):
        zero = jnp.zeros_like(x)
        count = x.shape[0]

        def at(q, t):
            if t < 0 or t >= rows:
                return zero
            return beyond[q, t] if (q, t) in beyond else a[q, t][0:count]

        return [at(p - 1, r), at(p + 1, r), at(p, r - 1), at(p, r + 1), lane_shift(x, -1), lane_shift(x, 1)]

    for p in range(-1, planes + 1):
        for r in range(rows):
            inside = 0 <= p < planes
            x = a[p, r] if inside else a[p, r][0:1]
            lanes = slice(p * rows * LANES + r * LANES, p * rows * LANES + (r + 1) * LANES)
            total = storage_coef
            for n, other in enumerate(near(x, p, r)):
                edge = 0.5 * (x + other)
                if inside:
                    w_ref[n, :, lanes] = edge
                    w0_ref[n : n + 1, lanes] = edge[0:1]
                total = total + edge[0:1]
            value = damping / total
            if not inside:
                value = jnp.where(beside[0 if p < 0 else 1] == 1, value, 0.0)
            inv_ref[p + 1 : p + 2, r * LANES : (r + 1) * LANES] = value


def all_weights(beside, coef, low, high):
    terms, planes, cy, cz = coef.shape
    cells = cy * cz
    return pl.pallas_call(
        weights_kernel,
        in_specs=[SMEM] + [VMEM] * 3,
        out_specs=[VMEM] * 3,
        out_shape=[
            jax.ShapeDtypeStruct((KINDS, terms, planes * cells), jnp.float32),
            jax.ShapeDtypeStruct((KINDS, planes * cells), jnp.float32),
            jax.ShapeDtypeStruct((planes + 2, cells), jnp.float32),
        ],
        compiler_params=pltpu.CompilerParams(vmem_limit_bytes=6 * 2**20),
        cost_estimate=pl.CostEstimate(flops=30 * coef.size, bytes_accessed=0, transcendentals=0),
    )(beside, coef.reshape(terms, planes * cy, cz), low, high)


def after(x, *others):
    others = [o for o in others if o is not None]
    return lax.optimization_barrier((x, *others))[0] if others else x


def gathered(halves, inner, outer):
    size = inner * outer
    ring = [(i, (i + inner) % size) for i in range(size)]
    turned = [(i, i // inner * inner + (i % inner + 1) % inner) for i in range(size)]
    found = []
    current = list(halves)
    for step in range(outer):
        sent = list(current)
        for h, block in enumerate(sent):
            found.append((block, step, 0, h))
            for turn in range(1, inner):
                block = lax.ppermute(block, "mode", turned)
                found.append((block, step, turn, h))
            if step < outer - 1:
                current[h] = after(lax.ppermute(sent[h], "mode", ring), block)
    return found


def on_device(pressure, source, coefficients, coupling):
    size, slabs = lax.axis_size("mode"), lax.axis_size("space")
    own, planes, cy, cz = pressure.shape
    cells = cy * cz
    terms = coefficients.shape[0]
    inner = max(1, LANES // own)
    outer = size // inner
    halves = 2 if own % 32 == 0 else 1
    rows = own // halves

    flat = pressure.reshape(own, planes * cells)
    press = [flat[h * rows : (h + 1) * rows] for h in range(halves)]
    found = gathered(press, inner, outer)
    mode_at = lax.axis_index("mode")
    outer_at, inner_at = mode_at // inner, mode_at % inner
    offsets = jnp.stack(
        [
            ((outer_at - f[1] + outer) % outer * inner + (inner_at - f[2] + inner) % inner) * own + f[3] * rows
            for f in found
        ]
    ).astype(jnp.int32)
    c = coupling.reshape(terms, halves, rows, size * own)

    coefficients = after(coefficients, found[inner - 1][0])
    source = after(source, found[2 * inner * halves][0])

    up = [(i, i + 1) for i in range(slabs - 1)]
    down = [(j, i) for i, j in up]
    low = lax.ppermute(jnp.concatenate([coefficients[:, planes - 1], coefficients[:1, planes - 2]]), "space", up)
    high = lax.ppermute(jnp.concatenate([coefficients[:, 0], coefficients[:1, 1]]), "space", down)
    slab = lax.axis_index("space")
    beside = jnp.stack([slab > 0, slab < slabs - 1]).astype(jnp.int32)
    w, w0, inv = all_weights(beside, coefficients, low, high)

    odd = (slab % 2).astype(jnp.int32).reshape(1)
    pairs = [[(i, i + 1) for i in range(start, slabs - 1, 2)] for start in (1, 0)]
    swap_odd, swap_even = [p + [(j, i) for i, j in p] for p in pairs]

    flat = source.reshape(own, planes * cells)
    src = [flat[h * rows : (h + 1) * rows] for h in range(halves)]
    for step in range(ITERS):
        blocks = [f[0] for f in found]
        states = []
        for h in range(halves):
            part, odd_own, even_own = mix(odd, offsets, blocks, c, w, press[h], src[h], h, planes)
            even_in = lax.ppermute(even_own, "space", swap_even)
            odd_in = lax.ppermute(odd_own, "space", swap_odd)
            states.append((part, press[h], odd_own, even_own, odd_in, even_in))
        if step < ITERS - 1:
            press = [smooth(odd, [state], w0, inv, False)[0] for state in states]
            found = gathered(press, inner, outer)
        else:
            outs = smooth(odd, states, w0, inv, True)
    return tuple(x.reshape(pressure.shape) for x in outs)


def solution(mesh):
    in_specs = (
        P("mode", "space", None, None),
        P("mode", "space", None, None),
        P(None, "space", None, None),
        P(None, "mode", None),
    )
    out_specs = (P("mode", "space", None, None), P("mode", "space", None, None))
    return jax.shard_map(
        on_device, mesh=mesh, in_specs=in_specs, out_specs=out_specs, check_vma=False
    )
```

```python
import jax
import jax.numpy as jnp
from jax import lax
from jax.experimental import pallas as pl
from jax.experimental.pallas import tpu as pltpu
from jax.sharding import PartitionSpec as P

ITERS = 2
LANES = 128
KINDS = 6

storage_coef = 1.0
damping = 0.7

VMEM = pl.BlockSpec(memory_space=pltpu.VMEM)
SMEM = pl.BlockSpec(memory_space=pltpu.SMEM)


def parts_of(x):
    hi = x.astype(jnp.bfloat16)
    return hi, (x - hi.astype(jnp.float32)).astype(jnp.bfloat16)


def place(u_ref, blocks, offsets):
    part = u_ref.shape[0] // 3
    for s, block in enumerate(blocks):
        rows = block.shape[0]
        hi, lo = parts_of(block[...])
        row = pl.multiple_of(offsets[s], rows)
        u_ref[pl.ds(row, rows), :] = hi
        u_ref[pl.ds(row + part, rows), :] = lo
        u_ref[pl.ds(row + 2 * part, rows), :] = hi


def lane_shift(x, offset):
    moved = pltpu.roll(x, (-offset) % LANES, 1)
    lane = lax.broadcasted_iota(jnp.int32, x.shape, 1)
    edge = 0 if offset < 0 else LANES - 1
    return jnp.where(lane == edge, 0.0, moved)


def mix_kernel(planes, count, odd, offsets, *refs):
    blocks, refs = refs[:count], refs[count:]
    c_ref, w_ref, press, source, part_ref, odd_ref, even_ref, field_ref, u_ref, cs_ref, sems = refs
    rows, lanes_all = press.shape
    cells = lanes_all // planes
    terms = w_ref.shape[1]
    chunk = terms // sems.shape[0]
    group = 32 if rows % 32 == 0 else rows

    copies = [
        pltpu.make_async_copy(
            c_ref.at[pl.ds(k, chunk)], cs_ref.at[pl.ds(k, chunk)], sems.at[k // chunk]
        )
        for k in range(0, terms, chunk)
    ]
    for copy in copies:
        copy.start()
    place(u_ref, blocks, offsets)
    tile = 2 * LANES if cells % (2 * LANES) == 0 else LANES

    def product(k, t):
        hi, lo = parts_of(cs_ref[k : k + chunk].reshape(chunk * rows, cs_ref.shape[2]))
        return jnp.dot(
            jnp.concatenate([hi, hi, lo], axis=1),
            u_ref[:, t * tile : (t + 1) * tile],
            preferred_element_type=jnp.float32,
        )

    def weigh(start, t, m):
        for r in range(tile // LANES):
            lanes = slice(t * tile + r * LANES, t * tile + (r + 1) * LANES)
            for g in range(0, rows, group):
                some = slice(g, g + group)
                total = [None if start == 0 else field_ref[n, some, lanes] for n in range(KINDS)]
                for k in range(chunk):
                    value = m[k * rows + g : k * rows + g + group, r * LANES : (r + 1) * LANES]
                    for n in range(KINDS):
                        term = w_ref[n, start + k : start + k + 1, lanes] * value
                        total[n] = term if total[n] is None else total[n] + term
                for n in range(KINDS):
                    field_ref[n, some, lanes] = total[n]

    before = None
    for k in range(0, terms, chunk):
        copies[k // chunk].wait()
        for t in range(lanes_all // tile):
            m = product(k, t)
            if before is not None:
                weigh(*before)
            before = (k, t, m)
    weigh(*before)

    count = cells // LANES
    for p in range(planes):
        for r in range(count):

            def field(n, p=p, r=r):
                return field_ref[n, :, p * cells + r * LANES : p * cells + (r + 1) * LANES]

            lanes = slice(p * cells + r * LANES, p * cells + (r + 1) * LANES)
            flux = field(0) + field(1) + field(2) + field(3)
            if p > 0:
                flux = flux - field(1, p - 1, r)
            if p < planes - 1:
                flux = flux - field(0, p + 1, r)
            if r > 0:
                flux = flux - field(3, p, r - 1)
            if r < count - 1:
                flux = flux - field(2, p, r + 1)
            below, above = field(4), field(5)
            flux = flux + (below - lane_shift(above, -1)) + (above - lane_shift(below, 1))
            part_ref[:, lanes] = source[:, lanes] - storage_coef * press[:, lanes] - flux

    lower, upper = slice(0, cells), slice((planes - 1) * cells, planes * cells)
    is_odd = odd[0] == 1
    for at, (low, high) in enumerate(
        [(part_ref[:, lower], part_ref[:, upper]), (field_ref[0, :, lower], field_ref[1, :, upper])]
    ):
        odd_ref[at] = jnp.where(is_odd, high, low)
        even_ref[at] = jnp.where(is_odd, low, high)


def mix(odd, offsets, blocks, c, w, press, source, planes):
    rows, lanes_all = press.shape
    cells = lanes_all // planes
    terms, _, modes = c.shape
    chunks = max(1, terms * rows // 256)
    sent = jax.ShapeDtypeStruct((2, rows, cells), jnp.float32)
    return pl.pallas_call(
        lambda *refs: mix_kernel(planes, len(blocks), *refs),
        in_specs=[SMEM] * 2 + [VMEM] * len(blocks) + [pl.BlockSpec(memory_space=pltpu.HBM)] + [VMEM] * 3,
        out_specs=[VMEM] * 3,
        out_shape=[jax.ShapeDtypeStruct(press.shape, jnp.float32), sent, sent],
        scratch_shapes=[
            pltpu.VMEM((KINDS, rows, lanes_all), jnp.float32),
            pltpu.VMEM((3 * modes, lanes_all), jnp.bfloat16),
            pltpu.VMEM((terms, rows, modes), jnp.float32),
            pltpu.SemaphoreType.DMA((chunks,)),
        ],
        compiler_params=pltpu.CompilerParams(vmem_limit_bytes=24 * 2**20),
        cost_estimate=pl.CostEstimate(
            flops=6 * terms * rows * modes * lanes_all, bytes_accessed=4 * terms * rows * modes, transcendentals=0
        ),
    )(odd, offsets, *blocks, c, w, press, source)


def smooth_kernel(planes, halves, final, odd, *refs):
    w_ref, inv_ref = refs[6 * halves : 6 * halves + 2]
    outs = refs[6 * halves + 2 :]
    is_odd = odd[0] == 1
    for h in range(halves):
        part, press, odd_own, even_own, odd_in, even_in = refs[6 * h : 6 * h + 6]
        rows, lanes_all = press.shape
        cells = lanes_all // planes
        count = cells // LANES

        def lanes(p, r):
            return slice(p * cells + r * LANES, p * cells + (r + 1) * LANES)

        res, first = {}, {}
        for r in range(count):
            row = slice(r * LANES, (r + 1) * LANES)
            for p in range(planes):
                res[p, r] = part[:, lanes(p, r)]
            res[0, r] = res[0, r] + jnp.where(is_odd, even_in[1, :, row], odd_in[1, :, row])
            res[planes - 1, r] = res[planes - 1, r] + jnp.where(is_odd, odd_in[1, :, row], even_in[1, :, row])
            odd_side = odd_in[0, :, row] + odd_own[1, :, row]
            even_side = even_in[0, :, row] + even_own[1, :, row]
            res[-1, r] = jnp.where(is_odd, even_side, odd_side)
            res[planes, r] = jnp.where(is_odd, odd_side, even_side)
            for p in range(-1, planes + 1):
                first[p, r] = inv_ref[p + 1 : p + 2, row] * res[p, r]
        for p in range(planes):
            for r in range(count):
                f = first[p, r]
                row = slice(r * LANES, (r + 1) * LANES)

                def w(n):
                    return w_ref[n : n + 1, lanes(p, r)]

                mean = storage_coef * f + w(0) * (f - first[p - 1, r]) + w(1) * (f - first[p + 1, r])
                mean = mean + w(2) * (f - first[p, r - 1] if r > 0 else f)
                mean = mean + w(3) * (f - first[p, r + 1] if r < count - 1 else f)
                mean = mean + w(4) * (f - lane_shift(f, -1)) + w(5) * (f - lane_shift(f, 1))
                second = f + inv_ref[p + 1 : p + 2, row] * (res[p, r] - mean)
                new = press[:, lanes(p, r)] + second
                if final:
                    outs[0][h * rows : (h + 1) * rows, p * count + r, :] = new
                    outs[1][h * rows : (h + 1) * rows, p * count + r, :] = res[p, r]
                else:
                    outs[h][:, lanes(p, r)] = new


def smooth(odd, states, w0, inv, final):
    halves = len(states)
    rows, lanes_all = states[0][1].shape
    planes = inv.shape[0] - 2
    if final:
        out_shape = [jax.ShapeDtypeStruct((halves * rows, lanes_all // LANES, LANES), jnp.float32)] * 2
    else:
        out_shape = [jax.ShapeDtypeStruct((rows, lanes_all), jnp.float32)] * halves
    return pl.pallas_call(
        lambda *refs: smooth_kernel(planes, halves, final, *refs),
        in_specs=[SMEM] + [VMEM] * (6 * halves + 2),
        out_specs=[VMEM] * len(out_shape),
        out_shape=out_shape,
        compiler_params=pltpu.CompilerParams(vmem_limit_bytes=8 * 2**20),
        cost_estimate=pl.CostEstimate(flops=40 * halves * rows * lanes_all, bytes_accessed=0, transcendentals=0),
    )(odd, *[x for state in states for x in state], w0, inv)


def weights_kernel(beside, coef_ref, low_ref, high_ref, w_ref, w0_ref, inv_ref):
    terms = coef_ref.shape[0]
    rows = low_ref.shape[1]
    planes = coef_ref.shape[1] // rows
    a = {(p, r): coef_ref[:, p * rows + r, :] for p in range(planes) for r in range(rows)}
    a.update({(-1, r): low_ref[0:terms, r, :] for r in range(rows)})
    a.update({(planes, r): high_ref[0:terms, r, :] for r in range(rows)})
    beyond = {(-2, r): low_ref[terms : terms + 1, r, :] for r in range(rows)}
    beyond.update({(planes + 1, r): high_ref[terms : terms + 1, r, :] for r in range(rows)})

    def near(x, p, r):
        zero = jnp.zeros_like(x)
        count = x.shape[0]

        def at(q, t):
            if t < 0 or t >= rows:
                return zero
            return beyond[q, t] if (q, t) in beyond else a[q, t][0:count]

        return [at(p - 1, r), at(p + 1, r), at(p, r - 1), at(p, r + 1), lane_shift(x, -1), lane_shift(x, 1)]

    for p in range(-1, planes + 1):
        for r in range(rows):
            inside = 0 <= p < planes
            x = a[p, r] if inside else a[p, r][0:1]
            lanes = slice(p * rows * LANES + r * LANES, p * rows * LANES + (r + 1) * LANES)
            total = storage_coef
            for n, other in enumerate(near(x, p, r)):
                edge = 0.5 * (x + other)
                if inside:
                    w_ref[n, :, lanes] = edge
                    w0_ref[n : n + 1, lanes] = edge[0:1]
                total = total + edge[0:1]
            value = damping / total
            if not inside:
                value = jnp.where(beside[0 if p < 0 else 1] == 1, value, 0.0)
            inv_ref[p + 1 : p + 2, r * LANES : (r + 1) * LANES] = value


def all_weights(beside, coef, low, high):
    terms, planes, cy, cz = coef.shape
    cells = cy * cz
    return pl.pallas_call(
        weights_kernel,
        in_specs=[SMEM] + [VMEM] * 3,
        out_specs=[VMEM] * 3,
        out_shape=[
            jax.ShapeDtypeStruct((KINDS, terms, planes * cells), jnp.float32),
            jax.ShapeDtypeStruct((KINDS, planes * cells), jnp.float32),
            jax.ShapeDtypeStruct((planes + 2, cells), jnp.float32),
        ],
        compiler_params=pltpu.CompilerParams(vmem_limit_bytes=6 * 2**20),
        cost_estimate=pl.CostEstimate(flops=30 * coef.size, bytes_accessed=0, transcendentals=0),
    )(beside, coef.reshape(terms, planes * cy, cz), low, high)


def after(x, *others):
    others = [o for o in others if o is not None]
    return lax.optimization_barrier((x, *others))[0] if others else x


def gathered(whole, halves, inner, outer):
    size = inner * outer
    rows = whole.shape[0] // halves
    ring = [(i, (i + inner) % size) for i in range(size)]
    turned = [(i, i // inner * inner + (i % inner + 1) % inner) for i in range(size)]
    found = []
    current = [whole[h * rows : (h + 1) * rows] for h in range(halves)]
    for step in range(outer):
        sent = list(current)
        for h, block in enumerate(sent):
            found.append((block, step, 0, h * rows))
            for turn in range(1, inner):
                block = lax.ppermute(block, "mode", turned)
                found.append((block, step, turn, h * rows))
            if step < outer - 1:
                current[h] = after(lax.ppermute(sent[h], "mode", ring), block)
    return found


def on_device(pressure, source, coefficients, coupling):
    size, slabs = lax.axis_size("mode"), lax.axis_size("space")
    own, planes, cy, cz = pressure.shape
    cells = cy * cz
    terms = coefficients.shape[0]
    inner = max(1, LANES // own)
    outer = size // inner
    halves = 2 if own % 32 == 0 else 1

    flat = pressure.reshape(own, planes * cells)
    press = flat
    found = gathered(press, halves, inner, outer)
    mode_at = lax.axis_index("mode")
    outer_at, inner_at = mode_at // inner, mode_at % inner
    offsets = jnp.stack(
        [
            ((outer_at - f[1] + outer) % outer * inner + (inner_at - f[2] + inner) % inner) * own + f[3]
            for f in found
        ]
    ).astype(jnp.int32)
    c = coupling

    coefficients = after(coefficients, found[inner - 1][0])
    source = after(source, found[2 * inner * halves][0])

    up = [(i, i + 1) for i in range(slabs - 1)]
    down = [(j, i) for i, j in up]
    low = lax.ppermute(jnp.concatenate([coefficients[:, planes - 1], coefficients[:1, planes - 2]]), "space", up)
    high = lax.ppermute(jnp.concatenate([coefficients[:, 0], coefficients[:1, 1]]), "space", down)
    slab = lax.axis_index("space")
    beside = jnp.stack([slab > 0, slab < slabs - 1]).astype(jnp.int32)
    beside = after(beside, found[-inner * halves][0])
    w, w0, inv = all_weights(beside, coefficients, low, high)

    odd = (slab % 2).astype(jnp.int32).reshape(1)
    pairs = [[(i, i + 1) for i in range(start, slabs - 1, 2)] for start in (1, 0)]
    swap_odd, swap_even = [p + [(j, i) for i, j in p] for p in pairs]

    src = source.reshape(own, planes * cells)
    for step in range(ITERS):
        part, odd_own, even_own = mix(odd, offsets, [f[0] for f in found], c, w, press, src, planes)
        odd_in = lax.ppermute(odd_own, "space", swap_odd)
        even_in = lax.ppermute(even_own, "space", swap_even)
        state = (part, press, odd_own, even_own, odd_in, even_in)
        if step < ITERS - 1:
            press = smooth(odd, [state], w0, inv, False)[0]
            found = gathered(press, halves, inner, outer)
        else:
            outs = smooth(odd, [state], w0, inv, True)
    return tuple(x.reshape(pressure.shape) for x in outs)


def solution(mesh):
    in_specs = (
        P("mode", "space", None, None),
        P("mode", "space", None, None),
        P(None, "space", None, None),
        P(None, "mode", None),
    )
    out_specs = (P("mode", "space", None, None), P("mode", "space", None, None))
    return jax.shard_map(
        on_device, mesh=mesh, in_specs=in_specs, out_specs=out_specs, check_vma=False
    )
```

```python
import jax
import jax.numpy as jnp
from jax import lax
from jax.experimental import pallas as pl
from jax.experimental.pallas import tpu as pltpu
from jax.sharding import PartitionSpec as P

ITERS = 2
LANES = 128
KINDS = 6

storage_coef = 1.0
damping = 0.7

VMEM = pl.BlockSpec(memory_space=pltpu.VMEM)
SMEM = pl.BlockSpec(memory_space=pltpu.SMEM)


def parts_of(x):
    hi = x.astype(jnp.bfloat16)
    return hi, (x - hi.astype(jnp.float32)).astype(jnp.bfloat16)


def place(u_ref, blocks, offsets):
    part = u_ref.shape[0] // 3
    for s, block in enumerate(blocks):
        rows = block.shape[0]
        hi, lo = parts_of(block[...])
        row = pl.multiple_of(offsets[s], rows)
        u_ref[pl.ds(row, rows), :] = hi
        u_ref[pl.ds(row + part, rows), :] = lo
        u_ref[pl.ds(row + 2 * part, rows), :] = hi


def lane_shift(x, offset):
    moved = pltpu.roll(x, (-offset) % LANES, 1)
    lane = lax.broadcasted_iota(jnp.int32, x.shape, 1)
    edge = 0 if offset < 0 else LANES - 1
    return jnp.where(lane == edge, 0.0, moved)


def mix_kernel(planes, count, odd, offsets, *refs):
    blocks, refs = refs[:count], refs[count:]
    c_ref, w_ref, press, source, part_ref, odd_ref, even_ref, field_ref, u_ref, cs_ref, sems = refs
    rows, lanes_all = press.shape
    cells = lanes_all // planes
    terms = w_ref.shape[1]
    chunk = terms // sems.shape[0]
    group = 32 if rows % 32 == 0 else rows

    copies = [
        pltpu.make_async_copy(
            c_ref.at[pl.ds(k, chunk)], cs_ref.at[pl.ds(k, chunk)], sems.at[k // chunk]
        )
        for k in range(0, terms, chunk)
    ]
    for copy in copies:
        copy.start()
    place(u_ref, blocks, offsets)
    tile = 2 * LANES if cells % (2 * LANES) == 0 else LANES

    def product(k, t):
        hi, lo = parts_of(cs_ref[k : k + chunk].reshape(chunk * rows, cs_ref.shape[2]))
        return jnp.dot(
            jnp.concatenate([hi, hi, lo], axis=1),
            u_ref[:, t * tile : (t + 1) * tile],
            preferred_element_type=jnp.float32,
        )

    def weigh(start, t, m):
        for r in range(tile // LANES):
            lanes = slice(t * tile + r * LANES, t * tile + (r + 1) * LANES)
            for g in range(0, rows, group):
                some = slice(g, g + group)
                total = [None if start == 0 else field_ref[n, some, lanes] for n in range(KINDS)]
                for k in range(chunk):
                    value = m[k * rows + g : k * rows + g + group, r * LANES : (r + 1) * LANES]
                    for n in range(KINDS):
                        term = w_ref[n, start + k : start + k + 1, lanes] * value
                        total[n] = term if total[n] is None else total[n] + term
                for n in range(KINDS):
                    field_ref[n, some, lanes] = total[n]

    before = None
    for k in range(0, terms, chunk):
        copies[k // chunk].wait()
        for t in range(lanes_all // tile):
            m = product(k, t)
            if before is not None:
                weigh(*before)
            before = (k, t, m)
    weigh(*before)

    count = cells // LANES
    for p in range(planes):
        for r in range(count):

            def field(n, p=p, r=r):
                return field_ref[n, :, p * cells + r * LANES : p * cells + (r + 1) * LANES]

            lanes = slice(p * cells + r * LANES, p * cells + (r + 1) * LANES)
            flux = field(0) + field(1) + field(2) + field(3)
            if p > 0:
                flux = flux - field(1, p - 1, r)
            if p < planes - 1:
                flux = flux - field(0, p + 1, r)
            if r > 0:
                flux = flux - field(3, p, r - 1)
            if r < count - 1:
                flux = flux - field(2, p, r + 1)
            below, above = field(4), field(5)
            flux = flux + (below - lane_shift(above, -1)) + (above - lane_shift(below, 1))
            part_ref[:, lanes] = source[:, lanes] - storage_coef * press[:, lanes] - flux

    lower, upper = slice(0, cells), slice((planes - 1) * cells, planes * cells)
    is_odd = odd[0] == 1
    for at, (low, high) in enumerate(
        [(part_ref[:, lower], part_ref[:, upper]), (field_ref[0, :, lower], field_ref[1, :, upper])]
    ):
        odd_ref[at] = jnp.where(is_odd, high, low)
        even_ref[at] = jnp.where(is_odd, low, high)


def mix(odd, offsets, blocks, c, w, press, source, planes):
    rows, lanes_all = press.shape
    cells = lanes_all // planes
    terms, _, modes = c.shape
    chunks = max(1, terms * rows // 512)
    sent = jax.ShapeDtypeStruct((2, rows, cells), jnp.float32)
    return pl.pallas_call(
        lambda *refs: mix_kernel(planes, len(blocks), *refs),
        in_specs=[SMEM] * 2 + [VMEM] * len(blocks) + [pl.BlockSpec(memory_space=pltpu.HBM)] + [VMEM] * 3,
        out_specs=[VMEM] * 3,
        out_shape=[jax.ShapeDtypeStruct(press.shape, jnp.float32), sent, sent],
        scratch_shapes=[
            pltpu.VMEM((KINDS, rows, lanes_all), jnp.float32),
            pltpu.VMEM((3 * modes, lanes_all), jnp.bfloat16),
            pltpu.VMEM((terms, rows, modes), jnp.float32),
            pltpu.SemaphoreType.DMA((chunks,)),
        ],
        compiler_params=pltpu.CompilerParams(vmem_limit_bytes=24 * 2**20),
        cost_estimate=pl.CostEstimate(
            flops=6 * terms * rows * modes * lanes_all, bytes_accessed=4 * terms * rows * modes, transcendentals=0
        ),
    )(odd, offsets, *blocks, c, w, press, source)


def smooth_kernel(planes, halves, final, odd, *refs):
    w_ref, inv_ref = refs[6 * halves : 6 * halves + 2]
    outs = refs[6 * halves + 2 :]
    is_odd = odd[0] == 1
    for h in range(halves):
        part, press, odd_own, even_own, odd_in, even_in = refs[6 * h : 6 * h + 6]
        rows, lanes_all = press.shape
        cells = lanes_all // planes
        count = cells // LANES

        def lanes(p, r):
            return slice(p * cells + r * LANES, p * cells + (r + 1) * LANES)

        res, first = {}, {}
        for r in range(count):
            row = slice(r * LANES, (r + 1) * LANES)
            for p in range(planes):
                res[p, r] = part[:, lanes(p, r)]
            res[0, r] = res[0, r] + jnp.where(is_odd, even_in[1, :, row], odd_in[1, :, row])
            res[planes - 1, r] = res[planes - 1, r] + jnp.where(is_odd, odd_in[1, :, row], even_in[1, :, row])
            odd_side = odd_in[0, :, row] + odd_own[1, :, row]
            even_side = even_in[0, :, row] + even_own[1, :, row]
            res[-1, r] = jnp.where(is_odd, even_side, odd_side)
            res[planes, r] = jnp.where(is_odd, odd_side, even_side)
            for p in range(-1, planes + 1):
                first[p, r] = inv_ref[p + 1 : p + 2, row] * res[p, r]
        for p in range(planes):
            for r in range(count):
                f = first[p, r]
                row = slice(r * LANES, (r + 1) * LANES)

                def w(n):
                    return w_ref[n : n + 1, lanes(p, r)]

                mean = storage_coef * f + w(0) * (f - first[p - 1, r]) + w(1) * (f - first[p + 1, r])
                mean = mean + w(2) * (f - first[p, r - 1] if r > 0 else f)
                mean = mean + w(3) * (f - first[p, r + 1] if r < count - 1 else f)
                mean = mean + w(4) * (f - lane_shift(f, -1)) + w(5) * (f - lane_shift(f, 1))
                second = f + inv_ref[p + 1 : p + 2, row] * (res[p, r] - mean)
                new = press[:, lanes(p, r)] + second
                if final:
                    outs[0][h * rows : (h + 1) * rows, p * count + r, :] = new
                    outs[1][h * rows : (h + 1) * rows, p * count + r, :] = res[p, r]
                else:
                    outs[h][:, lanes(p, r)] = new


def smooth(odd, states, w0, inv, final):
    halves = len(states)
    rows, lanes_all = states[0][1].shape
    planes = inv.shape[0] - 2
    if final:
        out_shape = [jax.ShapeDtypeStruct((halves * rows, lanes_all // LANES, LANES), jnp.float32)] * 2
    else:
        out_shape = [jax.ShapeDtypeStruct((rows, lanes_all), jnp.float32)] * halves
    return pl.pallas_call(
        lambda *refs: smooth_kernel(planes, halves, final, *refs),
        in_specs=[SMEM] + [VMEM] * (6 * halves + 2),
        out_specs=[VMEM] * len(out_shape),
        out_shape=out_shape,
        compiler_params=pltpu.CompilerParams(vmem_limit_bytes=8 * 2**20),
        cost_estimate=pl.CostEstimate(flops=40 * halves * rows * lanes_all, bytes_accessed=0, transcendentals=0),
    )(odd, *[x for state in states for x in state], w0, inv)


def weights_kernel(beside, coef_ref, low_ref, high_ref, w_ref, w0_ref, inv_ref):
    terms = coef_ref.shape[0]
    rows = low_ref.shape[1]
    planes = coef_ref.shape[1] // rows
    a = {(p, r): coef_ref[:, p * rows + r, :] for p in range(planes) for r in range(rows)}
    a.update({(-1, r): low_ref[0:terms, r, :] for r in range(rows)})
    a.update({(planes, r): high_ref[0:terms, r, :] for r in range(rows)})
    beyond = {(-2, r): low_ref[terms : terms + 1, r, :] for r in range(rows)}
    beyond.update({(planes + 1, r): high_ref[terms : terms + 1, r, :] for r in range(rows)})

    def near(x, p, r):
        zero = jnp.zeros_like(x)
        count = x.shape[0]

        def at(q, t):
            if t < 0 or t >= rows:
                return zero
            return beyond[q, t] if (q, t) in beyond else a[q, t][0:count]

        return [at(p - 1, r), at(p + 1, r), at(p, r - 1), at(p, r + 1), lane_shift(x, -1), lane_shift(x, 1)]

    for p in range(-1, planes + 1):
        for r in range(rows):
            inside = 0 <= p < planes
            x = a[p, r] if inside else a[p, r][0:1]
            lanes = slice(p * rows * LANES + r * LANES, p * rows * LANES + (r + 1) * LANES)
            total = storage_coef
            for n, other in enumerate(near(x, p, r)):
                edge = 0.5 * (x + other)
                if inside:
                    w_ref[n, :, lanes] = edge
                    w0_ref[n : n + 1, lanes] = edge[0:1]
                total = total + edge[0:1]
            value = damping / total
            if not inside:
                value = jnp.where(beside[0 if p < 0 else 1] == 1, value, 0.0)
            inv_ref[p + 1 : p + 2, r * LANES : (r + 1) * LANES] = value


def all_weights(beside, coef, low, high):
    terms, planes, cy, cz = coef.shape
    cells = cy * cz
    return pl.pallas_call(
        weights_kernel,
        in_specs=[SMEM] + [VMEM] * 3,
        out_specs=[VMEM] * 3,
        out_shape=[
            jax.ShapeDtypeStruct((KINDS, terms, planes * cells), jnp.float32),
            jax.ShapeDtypeStruct((KINDS, planes * cells), jnp.float32),
            jax.ShapeDtypeStruct((planes + 2, cells), jnp.float32),
        ],
        compiler_params=pltpu.CompilerParams(vmem_limit_bytes=6 * 2**20),
        cost_estimate=pl.CostEstimate(flops=30 * coef.size, bytes_accessed=0, transcendentals=0),
    )(beside, coef.reshape(terms, planes * cy, cz), low, high)


def after(x, *others):
    others = [o for o in others if o is not None]
    return lax.optimization_barrier((x, *others))[0] if others else x


def gathered(whole, halves, inner, outer):
    size = inner * outer
    rows = whole.shape[0] // halves
    ring = [(i, (i + inner) % size) for i in range(size)]
    turned = [(i, i // inner * inner + (i % inner + 1) % inner) for i in range(size)]
    found = []
    current = [whole[h * rows : (h + 1) * rows] for h in range(halves)]
    for step in range(outer):
        sent = list(current)
        for h, block in enumerate(sent):
            found.append((block, step, 0, h * rows))
            for turn in range(1, inner):
                block = lax.ppermute(block, "mode", turned)
                found.append((block, step, turn, h * rows))
            if step < outer - 1:
                current[h] = after(lax.ppermute(sent[h], "mode", ring), block)
    return found


def on_device(pressure, source, coefficients, coupling):
    size, slabs = lax.axis_size("mode"), lax.axis_size("space")
    own, planes, cy, cz = pressure.shape
    cells = cy * cz
    terms = coefficients.shape[0]
    inner = max(1, LANES // own)
    outer = size // inner
    halves = 2 if own % 32 == 0 else 1

    flat = pressure.reshape(own, planes * cells)
    press = flat
    found = gathered(press, halves, inner, outer)
    mode_at = lax.axis_index("mode")
    outer_at, inner_at = mode_at // inner, mode_at % inner
    offsets = jnp.stack(
        [
            ((outer_at - f[1] + outer) % outer * inner + (inner_at - f[2] + inner) % inner) * own + f[3]
            for f in found
        ]
    ).astype(jnp.int32)
    c = coupling

    coefficients = after(coefficients, found[inner - 1][0])
    source = after(source, found[2 * inner * halves][0])

    up = [(i, i + 1) for i in range(slabs - 1)]
    down = [(j, i) for i, j in up]
    low = lax.ppermute(jnp.concatenate([coefficients[:, planes - 1], coefficients[:1, planes - 2]]), "space", up)
    high = lax.ppermute(jnp.concatenate([coefficients[:, 0], coefficients[:1, 1]]), "space", down)
    slab = lax.axis_index("space")
    beside = jnp.stack([slab > 0, slab < slabs - 1]).astype(jnp.int32)
    beside = after(beside, found[-inner * halves][0])
    w, w0, inv = all_weights(beside, coefficients, low, high)

    odd = (slab % 2).astype(jnp.int32).reshape(1)
    pairs = [[(i, i + 1) for i in range(start, slabs - 1, 2)] for start in (1, 0)]
    swap_odd, swap_even = [p + [(j, i) for i, j in p] for p in pairs]

    src = source.reshape(own, planes * cells)
    for step in range(ITERS):
        part, odd_own, even_own = mix(odd, offsets, [f[0] for f in found], c, w, press, src, planes)
        odd_in = lax.ppermute(odd_own, "space", swap_odd)
        even_in = lax.ppermute(even_own, "space", swap_even)
        state = (part, press, odd_own, even_own, odd_in, even_in)
        if step < ITERS - 1:
            press = smooth(odd, [state], w0, inv, False)[0]
            found = gathered(press, halves, inner, outer)
        else:
            outs = smooth(odd, [state], w0, inv, True)
    return tuple(x.reshape(pressure.shape) for x in outs)


def solution(mesh):
    in_specs = (
        P("mode", "space", None, None),
        P("mode", "space", None, None),
        P(None, "space", None, None),
        P(None, "mode", None),
    )
    out_specs = (P("mode", "space", None, None), P("mode", "space", None, None))
    return jax.shard_map(
        on_device, mesh=mesh, in_specs=in_specs, out_specs=out_specs, check_vma=False
    )
```
